256 devices in a mesh: row: 32 (over x, z_lo, core), col: 8 (over y, z_hi).
Axes of the slice: x: 4, y: 4, z: 8 (z_hi: 2, z_lo: 4; z = z_hi * 4 + z_lo), core: 2. Of those that a mesh axis runs over, the one named last changes fastest.
Arguments:
- root_inverse: float32 [4096, 4096], P('row', 'col'), as said below
- factor_blocks: float32 [2, 4096, 2048], P(None, 'row', 'col'), may hold values from -0.1875 to 0.1875
- pattern: int32 [2, 32], replicated, may hold values 0 or 1
- diag_inverse: float32 [2, 2048, 2048], P(None, 'row', 'col'), may hold values from -0.6 to 0.6
Outputs:
- cross_inverse: float32 [2, 4096, 2048], P(None, 'row', 'col')
- diag_block_inverse: float32 [2, 2048, 2048], P(None, 'row', 'col')
The draws below stay inside these ranges and needn't reach their ends.
Inputs may be any that keep to these rules, and one draw needn't show every extreme that they name: root_inverse is symmetric.
All inputs are finite; a program needn't handle non-finite values.
Results may differ from the reference program's by a relative error of at most 0.000098.
Values sent between devices are 32-bit elements; how exact they have to be, the bound alone decides.
No kernel may reach another device: no remote copies, remote signals or barrier semaphores. Data moves between devices by JAX's collectives and lax.ppermute only.
A program may use at most 64 MiB of HBM per device.

```python
import math
import jax
import jax.numpy as jnp
from jax import lax

W0 = 4096
W1 = 2048
BLK = 128
CHILDREN = 2
NBLK = 32


def draw_root_inverse(key, part):
    key = jax.random.fold_in(key, 11)
    entry_key = jax.random.fold_in(key, 0)
    entries = jax.random.normal(entry_key, (W0, W0), jnp.float32)
    coupling = (entries + entries.T) * (0.35355339 / math.sqrt(W0))
    identity = (jnp.arange(W0)[:, None] == jnp.arange(W0)[None, :]).astype(jnp.float32)
    return 2.0 * (identity + coupling)


def plant(result, stream_key, low, high):
    extent = result.shape
    place = [jax.random.randint(jax.random.fold_in(stream_key, axis), (), 0, extent[axis]) for axis in range(len(extent))]
    result = result.at[tuple(place)].set(low)
    longest = extent.index(max(extent))
    place[longest] = (place[longest] + 1) % extent[longest]
    return result.at[tuple(place)].set(high)


def shard_levels(stream_key, shape, cuts, low, high):
    def one(axis_at, blocks):
        draws = jax.random.uniform(jax.random.fold_in(jax.random.fold_in(stream_key, 6), axis_at), (blocks,), jnp.float32, low / len(cuts), high / len(cuts))
        return jnp.repeat(jnp.exp(draws), shape[axis_at] // blocks).reshape((-1,) + (1,) * (len(shape) - axis_at - 1))

    gain = one(*cuts[0])
    for cut in cuts[1:]:
        gain = gain * one(*cut)
    return gain


def scatter_about(rng, extent, spread, most, cuts=(), dtype=jnp.bfloat16):
    values = spread * jax.random.normal(rng, extent, jnp.float32)
    if cuts:
        values = values * shard_levels(rng, extent, cuts, -0.22, 0.18)
    return jnp.clip(values, -most, most).astype(dtype)


def setup_inputs(seed: int = 0) -> dict:
    key_list = jax.random.split(jax.random.key(seed), 5)
    return {
        "root_inverse": draw_root_inverse(jax.random.fold_in(key_list[4], 71), 0),
        "factor_blocks": scatter_about(key_list[1], (CHILDREN, W0, W1), (W0 // 4) ** -0.5, 0.1875, ((1, 32), (2, 8)), jnp.float32),
        "pattern": plant((jax.random.randint(key_list[2], (CHILDREN, NBLK), 0, 2) < 1).astype(jnp.int32), jax.random.fold_in(key_list[2], 1), 0, 1),
        "diag_inverse": scatter_about(key_list[3], (CHILDREN, W1, W1), 0.1, 0.6, ((1, 32), (2, 8)), jnp.float32),
    }


def reference(root_inverse, factor_blocks, pattern, diag_inverse):
    row_pattern = jnp.repeat(pattern.astype(jnp.float32), BLK, axis=1)
    factor = factor_blocks * row_pattern[:, :, None]
    product = jnp.einsum("ik,jkc->jic", root_inverse, factor, precision=lax.Precision.HIGHEST)
    cross_inverse = -product * row_pattern[:, :, None]
    diag_block_inverse = diag_inverse - jnp.einsum("jkn,jkc->jnc", cross_inverse, factor, precision=lax.Precision.HIGHEST)
    return cross_inverse, diag_block_inverse
```

```python
import jax
import jax.numpy as jnp
from jax import lax
from jax.experimental import pallas as pl
from jax.experimental.pallas import tpu as pltpu
from jax.sharding import PartitionSpec as P

AX = ("row", "col")
BLK = 128
NX, NZL, NC, NY, NZH = 4, 4, 2, 4, 2


def linear(x, zl, c, y, zh):
    return (((x * NZL + zl) * NC + c) * NY + y) * NZH + zh


def moves(target):
    pairs = []
    for x in range(NX):
        for zl in range(NZL):
            for c in range(NC):
                for y in range(NY):
                    for zh in range(NZH):
                        pairs.append((linear(x, zl, c, y, zh), linear(*target(x, zl, c, y, zh))))
    return pairs


def z_step(d):
    def target(x, zl, c, y, zh):
        z = (zh * NZL + zl + d) % (NZL * NZH)
        return x, z % NZL, c, y, z // NZL

    return moves(target)


Z_UP, Z_DOWN = z_step(1), z_step(-1)
X_UP = moves(lambda x, zl, c, y, zh: ((x + 1) % NX, zl, c, y, zh))
X_DOWN = moves(lambda x, zl, c, y, zh: ((x - 1) % NX, zl, c, y, zh))
Y_1 = moves(lambda x, zl, c, y, zh: (x, zl, c, y ^ 1, zh))
Y_3 = moves(lambda x, zl, c, y, zh: (x, zl, c, y ^ 3, zh))
CORE = moves(lambda x, zl, c, y, zh: (x, zl, 1 - c, y, zh))
TURN = moves(lambda x, zl, c, y, zh: (zl, y, c, x, zh))
SWAP = moves(lambda x, zl, c, y, zh: (x, y, c, zl, zh))


def home(t):
    return moves(lambda x, zl, c, y, zh: (y, (x + t) % NX, c, zl, zh))


HOME = [home(t) for t in range(NX)]


def send(value, pairs):
    return lax.ppermute(value, AX, pairs)


def ring_blocks(block):
    half = block.shape[0] // 2
    up, down = [block], [block]
    for _ in range(3):
        up.append(send(up[-1], Z_UP))
        down.append(send(down[-1], Z_DOWN))
    top = send(up[3][:half], Z_UP)
    bottom = send(down[3][half:], Z_DOWN)
    return [block, down[1], down[2], down[3], top, bottom, up[3], up[2], up[1]]


def split(v):
    hi = v.astype(jnp.bfloat16)
    return hi, (v - hi.astype(jnp.float32)).astype(jnp.bfloat16)


def dot3(a, b, dims):
    def one(p, q):
        return lax.dot_general(p, q, (dims, ((), ())), preferred_element_type=jnp.float32)

    return one(a[0], b[0]) + (one(a[0], b[1]) + one(a[1], b[0]))


def cross_kernel(at, r0, r1, r2, r3, r4t, r4b, r5, r6, r7, *rest):
    own, other = rest[:5], rest[5:10]
    send_a, send_b, keep_a, keep_b, hi, lo, total = rest[10:]
    x, y, z, c = at[0], at[1], at[2], at[3]
    half = BLK // 2
    for refs, core in ((own, c), (other, 1 - c)):
        for ref, shift, skip in zip(refs, (0, 3, 1, 2, 2), (0, 0, 0, 0, half)):
            rows = ref.shape[0]
            start = pl.multiple_of((lax.rem(x + shift, 4) * 2 + core) * BLK + skip, half)
            hi[pl.ds(start, rows), :], lo[pl.ds(start, rows), :] = split(ref[...])
    blocks = [(r0, None), (r1, None), (r2, None), (r3, None), (r4t, r4b), (r5, None), (r6, None), (r7, None)]

    def product(d):
        place = lax.rem(z + d, 8)
        start = pl.multiple_of(lax.div(place, 4) * 4 * BLK, 4 * BLK)
        f = hi[pl.ds(start, 4 * BLK), :], lo[pl.ds(start, 4 * BLK), :]
        first, second = blocks[d]
        value = first[...] if second is None else jnp.concatenate([first[...], second[...]], axis=0)
        return dot3(split(value), f, ((1,), (0,)))

    for p in range(4):
        total[lax.rem(z + p, 4)] = product(p) + product(p + 4)
    cols = total.shape[2] // 2
    for ref, child, picks in ((send_a, 0, (1, 2)), (send_b, 1, (3, 2)), (keep_a, 0, (0, 3)), (keep_b, 1, (0, 1))):
        for slot, q in enumerate(picks):
            ref[slot] = total[y ^ q, :, child * cols : (child + 1) * cols]


def diag_kernel(at, e0, e1, e2, e3, e4t, e4b, e5, e6, e7, ga, ha, ka, gb, hb, kb, out_send, out_keep, fh, fl, gh, gl, total):
    y, z, c = at[1], at[2], at[3]
    half = BLK // 2
    for ref, d, skip in ((e0, 0, 0), (e1, 1, 0), (e2, 2, 0), (e3, 3, 0), (e4t, 4, 0), (e4b, 4, half), (e5, 5, 0), (e6, 6, 0), (e7, 7, 0)):
        place = lax.rem(z + d, 8)
        rows = pl.ds(pl.multiple_of(place * BLK + skip, half), ref.shape[0])
        fh[rows, :], fl[rows, :] = split(ref[...])
    cols = ga.shape[1]
    for child, blocks in ((0, ((ga[...], 0), (ha[...], 3), (ka[0], 1), (ka[1], 2))), (1, ((gb[...], 0), (hb[...], 1), (kb[0], 3), (kb[1], 2)))):
        for value, q in blocks:
            rows = pl.ds(pl.multiple_of((y ^ q) * BLK, BLK), BLK)
            here = slice(child * cols, (child + 1) * cols)
            gh[rows, here], gl[rows, here] = split(value)
    for child in range(2):
        here = slice(child * cols, (child + 1) * cols)
        g = gh[:, here], gl[:, here]
        for h in range(2):
            rows = slice(h * 4 * BLK, (h + 1) * 4 * BLK)
            total[h * cols : (h + 1) * cols, :] = dot3((fh[rows, here], fl[rows, here]), g, ((0,), (0,)))
        for s in range(4):
            out_keep[s, child] = total[pl.ds(pl.multiple_of(s * BLK + c * half, half), half), :]
            out_send[s, child] = total[pl.ds(pl.multiple_of(s * BLK + (1 - c) * half, half), half), :]


def local_call(kernel, at, operands, outs, scratch, flops):
    vmem = pl.BlockSpec(memory_space=pltpu.VMEM)
    return pl.pallas_call(
        kernel,
        out_shape=[jax.ShapeDtypeStruct(s, jnp.float32) for s in outs],
        in_specs=[pl.BlockSpec(memory_space=pltpu.SMEM)] + [vmem] * len(operands),
        out_specs=[vmem] * len(outs),
        scratch_shapes=scratch,
        cost_estimate=pl.CostEstimate(flops=flops, bytes_accessed=6 * 2**20, transcendentals=0),
        compiler_params=pltpu.CompilerParams(vmem_limit_bytes=32 * 2**20),
    )(at, *operands)


def body(root_inverse, factor_blocks, pattern, diag_inverse):
    row, col = lax.axis_index("row"), lax.axis_index("col")
    x, zl, c, y, zh = row // 8, (row // 2) % 4, row % 2, col // 2, col % 2
    at = jnp.stack([x, y, zh * 4 + zl, c]).astype(jnp.int32)
    weight = lax.dynamic_index_in_dim(pattern, row, 1, keepdims=False).astype(jnp.float32)
    cols = factor_blocks.shape[2]
    factor = jnp.concatenate([factor_blocks[0] * weight[0], factor_blocks[1] * weight[1]], axis=1)

    turned = send(factor, TURN)
    root = ring_blocks(root_inverse)
    f_up, f_down = send(turned, X_UP), send(turned, X_DOWN)
    far_top, far_bottom = send(f_up[: BLK // 2], X_UP), send(f_down[BLK // 2 :], X_DOWN)
    own = [turned, f_up, f_down, far_top, far_bottom]
    other = [send(v, CORE) for v in own]
    wide = (8 * BLK, 2 * cols)
    send_a, send_b, keep_a, keep_b = local_call(
        cross_kernel,
        at,
        root + own + other,
        [(2, BLK, cols)] * 4,
        [pltpu.VMEM(wide, jnp.bfloat16), pltpu.VMEM(wide, jnp.bfloat16), pltpu.VMEM((4, BLK, 2 * cols), jnp.float32)],
        6 * 512 * 1024 * 512,
    )
    sum_a, sum_b = keep_a + send(send_a, Y_1), keep_b + send(send_b, Y_3)
    g_a, g_b = sum_a[0] + send(sum_a[1], Y_3), sum_b[0] + send(sum_b[1], Y_1)
    crossed = send(jnp.stack([g_a, g_b]), SWAP)
    h_a, h_b = send(g_a, Y_3), send(g_b, Y_1)
    k_a, k_b = send(jnp.stack([g_a, h_a]), Y_1), send(jnp.stack([g_b, h_b]), Y_3)

    around = ring_blocks(factor)
    out_send, out_keep = local_call(
        diag_kernel,
        at,
        around + [g_a, h_a, k_a, g_b, h_b, k_b],
        [(4, 2, BLK // 2, cols)] * 2,
        [pltpu.VMEM(wide, jnp.bfloat16), pltpu.VMEM(wide, jnp.bfloat16)]
        + [pltpu.VMEM((4 * BLK, 2 * cols), jnp.bfloat16)] * 2
        + [pltpu.VMEM((4 * BLK, cols), jnp.float32)],
        6 * 512 * 512 * 512,
    )
    part = out_keep + send(out_send, CORE)
    diag = diag_inverse
    for t in range(4):
        diag = diag + send(lax.dynamic_index_in_dim(part, (x + t) % 4, 0, keepdims=False), HOME[t])
    return -crossed * weight[:, None, None], diag


def solution(mesh):
    placed = (P("row", "col"), P(None, "row", "col"), P(), P(None, "row", "col"))
    return jax.shard_map(
        body,
        mesh=mesh,
        in_specs=placed,
        out_specs=(P(None, "row", "col"), P(None, "row", "col")),
        check_vma=False,
    )
```

```python
import jax
import jax.numpy as jnp
from jax import lax
from jax.experimental import pallas as pl
from jax.experimental.pallas import tpu as pltpu
from jax.sharding import PartitionSpec as P

AX = ("row", "col")
BLK = 128
NX, NZL, NC, NY, NZH = 4, 4, 2, 4, 2


def linear(x, zl, c, y, zh):
    return (((x * NZL + zl) * NC + c) * NY + y) * NZH + zh


def moves(target):
    pairs = []
    for x in range(NX):
        for zl in range(NZL):
            for c in range(NC):
                for y in range(NY):
                    for zh in range(NZH):
                        pairs.append((linear(x, zl, c, y, zh), linear(*target(x, zl, c, y, zh))))
    return pairs


def z_step(d):
    def target(x, zl, c, y, zh):
        z = (zh * NZL + zl + d) % (NZL * NZH)
        return x, z % NZL, c, y, z // NZL

    return moves(target)


Z_UP, Z_DOWN = z_step(1), z_step(-1)
Z_MOVES = [moves(lambda x, zl, c, y, zh, d=d: (x, (zl + d) % NZL, c, y, zh)) for d in range(NZL)]
X_1 = moves(lambda x, zl, c, y, zh: (x ^ 1, zl, c, y, zh))
X_3 = moves(lambda x, zl, c, y, zh: (x ^ 3, zl, c, y, zh))
Y_1 = moves(lambda x, zl, c, y, zh: (x, zl, c, y ^ 1, zh))
Y_3 = moves(lambda x, zl, c, y, zh: (x, zl, c, y ^ 3, zh))
CORE = moves(lambda x, zl, c, y, zh: (x, zl, 1 - c, y, zh))
CROSS = [moves(lambda x, zl, c, y, zh, t=t: ((y + t) % NX, zl, c, x, zh)) for t in range(NX)]
HOME = moves(lambda x, zl, c, y, zh: (x, (zh * NZL + zl) >> 1, zl & 1, y, c))


def send(value, pairs):
    return lax.ppermute(value, AX, pairs)


def ring_blocks(block):
    half = block.shape[0] // 2
    up, down = [block], [block]
    for _ in range(3):
        up.append(send(up[-1], Z_UP))
        down.append(send(down[-1], Z_DOWN))
    top = send(up[3][:half], Z_UP)
    bottom = send(down[3][half:], Z_DOWN)
    return [block, down[1], down[2], down[3], top, bottom, up[3], up[2], up[1]]


def split(v):
    hi = v.astype(jnp.bfloat16)
    return hi, (v - hi.astype(jnp.float32)).astype(jnp.bfloat16)


def dot3(a, b, dims):
    def one(p, q):
        return lax.dot_general(p, q, (dims, ((), ())), preferred_element_type=jnp.float32)

    return one(a[0], b[0]) + (one(a[0], b[1]) + one(a[1], b[0]))


def factor_kernel(at, pattern, blocks, factor, p0, p1, p2, p3, pieces):
    row, zl = at[4], at[5]
    cols = blocks.shape[2]
    for child in range(2):
        weight = pattern[child, row].astype(jnp.float32)
        masked = blocks[child] * weight
        factor[:, child * cols : (child + 1) * cols] = masked
        for q in range(4):
            pieces[q, :, child * 64 : (child + 1) * 64] = masked[:, q * 64 : (q + 1) * 64]
    for d, ref in enumerate((p0, p1, p2, p3)):
        ref[...] = pieces[(zl + d) & 3]


def cross_kernel(at, r0, r1, r2, r3, r4t, r4b, r5, r6, r7, o0, o1, o2, o3, s0, s1, s2, s3, send_a, send_b, keep_a, keep_b, hi, lo, total):
    x, y, z, c, zl = at[0], at[1], at[2], at[3], at[5]
    for t, (own, other) in enumerate(((o0, s0), (o1, s1), (o2, s2), (o3, s3))):
        here = slice(t * BLK, (t + 1) * BLK)
        for ref, core in ((own, c), (other, 1 - c)):
            for d in range(4):
                rows = pl.ds(pl.multiple_of((((zl - d) & 3) * 2 + core) * BLK, BLK), BLK)
                hi[rows, here], lo[rows, here] = split(ref[d])
    blocks = [(r0, None), (r1, None), (r2, None), (r3, None), (r4t, r4b), (r5, None), (r6, None), (r7, None)]

    def product(d):
        place = (z + d) & 7
        start = pl.multiple_of((place >> 2) * (4 * BLK), 4 * BLK)
        f = hi[pl.ds(start, 4 * BLK), :], lo[pl.ds(start, 4 * BLK), :]
        first, second = blocks[d]
        value = first[...] if second is None else jnp.concatenate([first[...], second[...]], axis=0)
        return dot3(split(value), f, ((1,), (0,)))

    for p in range(4):
        value = product(p) + product(p + 4)
        rows = pl.ds(pl.multiple_of(((z + p) & 3) * BLK, BLK), BLK)
        for t in range(4):
            total[t, rows, :] = value[:, t * BLK : (t + 1) * BLK]
    for ref, part, picks in ((send_a, 0, (1, 2)), (send_b, 1, (3, 2)), (keep_a, 0, (0, 3)), (keep_b, 1, (0, 1))):
        for slot, q in enumerate(picks):
            ref[slot] = total[(x - (y ^ q)) & 3, part * 2 * BLK : (part + 1) * 2 * BLK, :]


def diag_kernel(at, e0, e1, e2, e3, e4t, e4b, e5, e6, e7, ga, ha, ka, gb, hb, kb, out_send, out_keep, fh, fl, gh, gl, total):
    x, y, z, c = at[0], at[1], at[2], at[3]
    half = BLK // 2
    for ref, d, skip in ((e0, 0, 0), (e1, 1, 0), (e2, 2, 0), (e3, 3, 0), (e4t, 4, 0), (e4b, 4, half), (e5, 5, 0), (e6, 6, 0), (e7, 7, 0)):
        rows = pl.ds(pl.multiple_of(((z + d) & 7) * BLK + skip, half), ref.shape[0])
        fh[rows, :], fl[rows, :] = split(ref[...])
    for part, blocks in ((0, ((ga[...], 0), (ha[...], 3), (ka[0], 1), (ka[1], 2))), (1, ((gb[...], 0), (hb[...], 1), (kb[0], 3), (kb[1], 2)))):
        rows = slice(part * 2 * BLK, (part + 1) * 2 * BLK)
        for value, q in blocks:
            h, l = split(value)
            for child in range(2):
                to = slice(child * 256 + q * 64, child * 256 + (q + 1) * 64)
                of = slice(child * 64, (child + 1) * 64)
                gh[rows, to], gl[rows, to] = h[:, of], l[:, of]
    for child in range(2):
        here = slice(child * 256, (child + 1) * 256)
        g = gh[:, here], gl[:, here]
        for h in range(2):
            rows = slice(h * 4 * BLK, (h + 1) * 4 * BLK)
            value = dot3(g, (fh[rows, here], fl[rows, here]), ((0,), (0,)))
            for q in range(4):
                total[child, h, q] = value[q * 64 : (q + 1) * 64, :]
    for slot, (child, r) in enumerate(((0, 1), (0, 2), (1, 3), (1, 2), (0, 0), (0, 3), (1, 0), (1, 1))):
        q = x ^ y ^ r
        out_keep[slot] = total[child, c, q]
        out_send[slot] = total[child, 1 - c, q]


def output_kernel(at, pattern, a0, a1, a2, a3, out, pieces):
    row, zl = at[4], at[5]
    for d, ref in enumerate((a0, a1, a2, a3)):
        pieces[(zl - d) & 3] = ref[...]
    for child in range(2):
        weight = pattern[child, row].astype(jnp.float32)
        for q in range(4):
            out[child, :, q * 64 : (q + 1) * 64] = -(pieces[q, :, child * 64 : (child + 1) * 64] * weight)


def local_call(kernel, scalars, operands, outs, scratch, flops, moved):
    vmem, smem = pl.BlockSpec(memory_space=pltpu.VMEM), pl.BlockSpec(memory_space=pltpu.SMEM)
    return pl.pallas_call(
        kernel,
        out_shape=[jax.ShapeDtypeStruct(s, jnp.float32) for s in outs],
        in_specs=[smem] * len(scalars) + [vmem] * len(operands),
        out_specs=[vmem] * len(outs),
        scratch_shapes=scratch,
        cost_estimate=pl.CostEstimate(flops=flops, bytes_accessed=moved, transcendentals=0),
        compiler_params=pltpu.CompilerParams(vmem_limit_bytes=32 * 2**20),
    )(*scalars, *operands)


def body(root_inverse, factor_blocks, pattern, diag_inverse):
    row, col = lax.axis_index("row"), lax.axis_index("col")
    x, zl, c, y, zh = row >> 3, (row >> 1) & 3, row & 1, col >> 1, col & 1
    at = jnp.stack([x, y, zh * 4 + zl, c, row, zl]).astype(jnp.int32)
    cols = factor_blocks.shape[2]
    piece = (BLK, BLK)

    root = ring_blocks(root_inverse)
    factor, *strips = local_call(
        factor_kernel, [at, pattern], [factor_blocks], [(BLK, 2 * cols)] + [piece] * 4, [pltpu.VMEM((4,) + piece, jnp.float32)], 2**16, 2**20
    )
    column = jnp.stack([strips[0]] + [send(strips[d], Z_MOVES[d]) for d in (1, 2, 3)])
    own = [send(column, CROSS[t]) for t in range(4)]
    other = [send(v, CORE) for v in own]
    wide = pltpu.VMEM((8 * BLK, 2 * cols), jnp.bfloat16)
    send_a, send_b, keep_a, keep_b = local_call(
        cross_kernel,
        [at],
        root + own + other,
        [(2, 2 * BLK, BLK)] * 4,
        [wide, wide, pltpu.VMEM((4, 4 * BLK, BLK), jnp.float32)],
        6 * 512 * 1024 * 512,
        6 * 2**20,
    )
    sum_a, sum_b = keep_a + send(send_a, Y_1), keep_b + send(send_b, Y_3)
    g_a, g_b = sum_a[0] + send(sum_a[1], Y_3), sum_b[0] + send(sum_b[1], Y_1)
    h_a, h_b = send(g_a, Y_3), send(g_b, Y_1)
    k_a, k_b = send(jnp.stack([g_a, h_a]), Y_1), send(jnp.stack([g_b, h_b]), Y_3)

    around = ring_blocks(factor)
    out_send, out_keep = local_call(
        diag_kernel,
        [at],
        around + [g_a, h_a, k_a, g_b, h_b, k_b],
        [(8, BLK // 2, cols)] * 2,
        [wide, wide]
        + [pltpu.VMEM((4 * BLK, 2 * cols), jnp.bfloat16)] * 2
        + [pltpu.VMEM((2, 2, 4, BLK // 2, cols), jnp.float32)],
        6 * 512 * 512 * 512,
        6 * 2**20,
    )
    part = out_keep + send(out_send, CORE)
    got_a, got_b = part[4:6] + send(part[:2], X_1), part[6:] + send(part[2:4], X_3)
    last = jnp.stack([got_a[0] + send(got_a[1], X_3), got_b[0] + send(got_b[1], X_1)])
    diag = diag_inverse + send(last, HOME)

    g = jnp.concatenate([g_a, g_b]).reshape((4,) + piece)
    rows = [lax.dynamic_index_in_dim(g, (zl + d) & 3, 0, keepdims=False) for d in range(4)]
    rows = [rows[0]] + [send(rows[d], Z_MOVES[d]) for d in (1, 2, 3)]
    (cross,) = local_call(output_kernel, [at, pattern], rows, [(2, BLK, cols)], [pltpu.VMEM((4,) + piece, jnp.float32)], 2**16, 2**20)
    return cross, diag


def solution(mesh):
    placed = (P("row", "col"), P(None, "row", "col"), P(), P(None, "row", "col"))
    return jax.shard_map(
        body,
        mesh=mesh,
        in_specs=placed,
        out_specs=(P(None, "row", "col"), P(None, "row", "col")),
        check_vma=False,
    )
```

```python
import jax
import jax.numpy as jnp
from jax import lax
from jax.experimental import pallas as pl
from jax.experimental.pallas import tpu as pltpu
from jax.sharding import PartitionSpec as P

AX = ("row", "col")
BLK = 128
NX, NZL, NC, NY, NZH = 4, 4, 2, 4, 2


def linear(x, zl, c, y, zh):
    return (((x * NZL + zl) * NC + c) * NY + y) * NZH + zh


def moves(target):
    pairs = []
    for x in range(NX):
        for zl in range(NZL):
            for c in range(NC):
                for y in range(NY):
                    for zh in range(NZH):
                        pairs.append((linear(x, zl, c, y, zh), linear(*target(x, zl, c, y, zh))))
    return pairs


def z_step(d):
    def target(x, zl, c, y, zh):
        z = (zh * NZL + zl + d) % (NZL * NZH)
        return x, z % NZL, c, y, z // NZL

    return moves(target)


Z_UP, Z_DOWN = z_step(1), z_step(-1)
Z_MOVES = [moves(lambda x, zl, c, y, zh, d=d: (x, (zl + d) % NZL, c, y, zh)) for d in range(NZL)]
X_MOVES = [moves(lambda x, zl, c, y, zh, d=d: ((x + d) % NX, zl, c, y, zh)) for d in range(NX)]
Y_MOVES = [moves(lambda x, zl, c, y, zh, d=d: (x, zl, c, (y + d) % NY, zh)) for d in range(NY)]
CORE = moves(lambda x, zl, c, y, zh: (x, zl, 1 - c, y, zh))
CROSS = [moves(lambda x, zl, c, y, zh, t=t: ((y + t) % NX, zl, c, x, zh)) for t in range(NX)]
HOME = moves(lambda x, zl, c, y, zh: (x, (zh * NZL + zl) >> 1, zl & 1, y, c))


def send(value, pairs):
    return lax.ppermute(value, AX, pairs)


def step(pair):
    return send(pair[0], Z_UP), send(pair[1], Z_DOWN)


def last_step(pair):
    half = pair[0].shape[0] // 2
    return send(pair[0][:half], Z_UP), send(pair[1][half:], Z_DOWN)


def in_order(block, one, two, three, four):
    return [block, one[1], two[1], three[1], four[0], four[1], three[0], two[0], one[0]]


def split(v):
    hi = v.astype(jnp.bfloat16)
    return hi, (v - hi.astype(jnp.float32)).astype(jnp.bfloat16)


def dot3(a, b, dims):
    def one(p, q):
        return lax.dot_general(p, q, (dims, ((), ())), preferred_element_type=jnp.float32)

    return one(a[0], b[0]) + (one(a[0], b[1]) + one(a[1], b[0]))


def factor_kernel(at, pattern, blocks, factor, p0, p1, p2, p3, pieces):
    row, zl = at[4], at[5]
    cols = blocks.shape[2]
    for child in range(2):
        weight = pattern[child, row].astype(jnp.float32)
        masked = blocks[child] * weight
        factor[:, child * cols : (child + 1) * cols] = masked
        for q in range(4):
            pieces[q, :, child * 64 : (child + 1) * 64] = masked[:, q * 64 : (q + 1) * 64]
    for d, ref in enumerate((p0, p1, p2, p3)):
        ref[...] = pieces[(zl + d) & 3]


def cross_kernel(at, r0, r1, r2, r3, r4t, r4b, r5, r6, r7, o0, o1, o2, o3, s0, s1, s2, s3, t0, t1, t2, t3, hi, lo, total):
    x, y, z, c, zl = at[0], at[1], at[2], at[3], at[5]
    for t, (own, other) in enumerate(((o0, s0), (o1, s1), (o2, s2), (o3, s3))):
        here = slice(t * BLK, (t + 1) * BLK)
        for ref, core in ((own, c), (other, 1 - c)):
            for d in range(4):
                rows = pl.ds(pl.multiple_of((((zl - d) & 3) * 2 + core) * BLK, BLK), BLK)
                hi[rows, here], lo[rows, here] = split(ref[d])
    blocks = [(r0, None), (r1, None), (r2, None), (r3, None), (r4t, r4b), (r5, None), (r6, None), (r7, None)]

    def product(d):
        place = (z + d) & 7
        start = pl.multiple_of((place >> 2) * (4 * BLK), 4 * BLK)
        f = hi[pl.ds(start, 4 * BLK), :], lo[pl.ds(start, 4 * BLK), :]
        first, second = blocks[d]
        value = first[...] if second is None else jnp.concatenate([first[...], second[...]], axis=0)
        return dot3(split(value), f, ((1,), (0,)))

    for p in range(4):
        value = product(p) + product(p + 4)
        rows = pl.ds(pl.multiple_of(((z + p) & 3) * BLK, BLK), BLK)
        for t in range(4):
            total[t, rows, :] = value[:, t * BLK : (t + 1) * BLK]
    for d, ref in enumerate((t0, t1, t2, t3)):
        ref[...] = total[(x - y - d) & 3]


def diag_kernel(at, e0, e1, e2, e3, e4t, e4b, e5, e6, e7, g0, g1, g2, g3, out_send, out_keep, fh, fl, gh, gl, total):
    x, y, z, c = at[0], at[1], at[2], at[3]
    half = BLK // 2
    for ref, d, skip in ((e0, 0, 0), (e1, 1, 0), (e2, 2, 0), (e3, 3, 0), (e4t, 4, 0), (e4b, 4, half), (e5, 5, 0), (e6, 6, 0), (e7, 7, 0)):
        rows = pl.ds(pl.multiple_of(((z + d) & 7) * BLK + skip, half), ref.shape[0])
        fh[rows, :], fl[rows, :] = split(ref[...])
    for d, ref in enumerate((g0, g1, g2, g3)):
        h, l = split(ref[...])
        for child in range(2):
            to = slice(child * 256 + d * 64, child * 256 + (d + 1) * 64)
            of = slice(child * 64, (child + 1) * 64)
            gh[:, to], gl[:, to] = h[:, of], l[:, of]
    for child in range(2):
        here = slice(child * 256, (child + 1) * 256)
        g = gh[:, here], gl[:, here]
        for h in range(2):
            rows = slice(h * 4 * BLK, (h + 1) * 4 * BLK)
            value = dot3(g, (fh[rows, here], fl[rows, here]), ((0,), (0,)))
            for d in range(4):
                total[h, d, child] = value[d * 64 : (d + 1) * 64, :]
    for t in range(4):
        d = (y - x - t) & 3
        out_keep[t] = total[c, d]
        out_send[t] = total[1 - c, d]


def output_kernel(at, pattern, a0, a1, a2, a3, out, pieces):
    row, zl = at[4], at[5]
    for d, ref in enumerate((a0, a1, a2, a3)):
        pieces[(zl - d) & 3] = ref[...]
    for child in range(2):
        weight = pattern[child, row].astype(jnp.float32)
        for q in range(4):
            out[child, :, q * 64 : (q + 1) * 64] = -(pieces[q, :, child * 64 : (child + 1) * 64] * weight)


def local_call(kernel, scalars, operands, outs, scratch, flops, moved):
    vmem, smem = pl.BlockSpec(memory_space=pltpu.VMEM), pl.BlockSpec(memory_space=pltpu.SMEM)
    return pl.pallas_call(
        kernel,
        out_shape=[jax.ShapeDtypeStruct(s, jnp.float32) for s in outs],
        in_specs=[smem] * len(scalars) + [vmem] * len(operands),
        out_specs=[vmem] * len(outs),
        scratch_shapes=scratch,
        cost_estimate=pl.CostEstimate(flops=flops, bytes_accessed=moved, transcendentals=0),
        compiler_params=pltpu.CompilerParams(vmem_limit_bytes=32 * 2**20),
    )(*scalars, *operands)


def body(root_inverse, factor_blocks, pattern, diag_inverse):
    row, col = lax.axis_index("row"), lax.axis_index("col")
    x, zl, c, y, zh = row >> 3, (row >> 1) & 3, row & 1, col >> 1, col & 1
    at = jnp.stack([x, y, zh * 4 + zl, c, row, zl]).astype(jnp.int32)
    cols = factor_blocks.shape[2]
    piece = (BLK, BLK)

    root1 = step((root_inverse, root_inverse))
    factor, *strips = local_call(
        factor_kernel, [at, pattern], [factor_blocks], [(BLK, 2 * cols)] + [piece] * 4, [pltpu.VMEM((4,) + piece, jnp.float32)], 2**16, 2**20
    )
    column = jnp.stack([strips[0]] + [send(strips[d], Z_MOVES[d]) for d in (1, 2, 3)])
    own = [send(column, CROSS[t]) for t in range(4)]
    other = [send(v, CORE) for v in own]
    around1 = step((factor, factor))
    root2 = step(root1)
    root2, around1 = lax.optimization_barrier((root2, around1))
    root3 = step(root2)
    root4 = last_step(root3)
    wide = pltpu.VMEM((8 * BLK, 2 * cols), jnp.bfloat16)
    parts = local_call(
        cross_kernel,
        [at],
        in_order(root_inverse, root1, root2, root3, root4) + own + other,
        [(4 * BLK, BLK)] * 4,
        [wide, wide, pltpu.VMEM((4, 4 * BLK, BLK), jnp.float32)],
        6 * 512 * 1024 * 512,
        6 * 2**20,
    )
    around2 = step(around1)
    g = parts[0] + send(parts[1], Y_MOVES[1]) + send(parts[2], Y_MOVES[2]) + send(parts[3], Y_MOVES[3])
    around3 = step(around2)
    gathered = [g] + [send(g, Y_MOVES[d]) for d in (1, 2, 3)]
    around4 = last_step(around3)

    out_send, out_keep = local_call(
        diag_kernel,
        [at],
        in_order(factor, around1, around2, around3, around4) + gathered,
        [(4, 2, BLK // 2, cols)] * 2,
        [wide, wide]
        + [pltpu.VMEM((4 * BLK, 2 * cols), jnp.bfloat16)] * 2
        + [pltpu.VMEM((2, 4, 2, BLK // 2, cols), jnp.float32)],
        6 * 512 * 512 * 512,
        6 * 2**20,
    )
    g_rows = g.reshape((4,) + piece)
    rows = [lax.dynamic_index_in_dim(g_rows, (zl + d) & 3, 0, keepdims=False) for d in range(4)]
    rows = [rows[0]] + [send(rows[d], Z_MOVES[d]) for d in (1, 2, 3)]
    swapped = send(out_send, CORE)
    out_keep, swapped, rows = lax.optimization_barrier((out_keep, swapped, rows))
    (cross,) = local_call(output_kernel, [at, pattern], rows, [(2, BLK, cols)], [pltpu.VMEM((4,) + piece, jnp.float32)], 2**16, 2**20)
    part = out_keep + swapped
    last = part[0] + send(part[1], X_MOVES[1]) + send(part[2], X_MOVES[2]) + send(part[3], X_MOVES[3])
    diag = diag_inverse + send(last, HOME)
    return cross, diag


def solution(mesh):
    placed = (P("row", "col"), P(None, "row", "col"), P(), P(None, "row", "col"))
    return jax.shard_map(
        body,
        mesh=mesh,
        in_specs=placed,
        out_specs=(P(None, "row", "col"), P(None, "row", "col")),
        check_vma=False,
    )
```

```python
import jax
import jax.numpy as jnp
from jax import lax
from jax.experimental import pallas as pl
from jax.experimental.pallas import tpu as pltpu
from jax.sharding import PartitionSpec as P

AX = ("row", "col")
BLK = 128
NX, NZL, NC, NY, NZH = 4, 4, 2, 4, 2


def linear(x, zl, c, y, zh):
    return (((x * NZL + zl) * NC + c) * NY + y) * NZH + zh


def moves(target):
    pairs = []
    for x in range(NX):
        for zl in range(NZL):
            for c in range(NC):
                for y in range(NY):
                    for zh in range(NZH):
                        pairs.append((linear(x, zl, c, y, zh), linear(*target(x, zl, c, y, zh))))
    return pairs


def z_step(d):
    def target(x, zl, c, y, zh):
        z = (zh * NZL + zl + d) % (NZL * NZH)
        return x, z % NZL, c, y, z // NZL

    return moves(target)


Z_UP, Z_DOWN = z_step(1), z_step(-1)
Z_MOVES = [moves(lambda x, zl, c, y, zh, d=d: (x, (zl + d) % NZL, c, y, zh)) for d in range(NZL)]
X_MOVES = [moves(lambda x, zl, c, y, zh, d=d: ((x + d) % NX, zl, c, y, zh)) for d in range(NX)]
Y_MOVES = [moves(lambda x, zl, c, y, zh, d=d: (x, zl, c, (y + d) % NY, zh)) for d in range(NY)]
CORE = moves(lambda x, zl, c, y, zh: (x, zl, 1 - c, y, zh))
CROSS = [moves(lambda x, zl, c, y, zh, t=t: ((y + t) % NX, zl, c, x, zh)) for t in range(NX)]
HOME = moves(lambda x, zl, c, y, zh: (x, (zh * NZL + zl) >> 1, zl & 1, y, c))


def send(value, pairs):
    return lax.ppermute(value, AX, pairs)


def step(pair):
    return send(pair[0], Z_UP), send(pair[1], Z_DOWN)


def last_step(pair):
    half = pair[0].shape[0] // 2
    return send(pair[0][:half], Z_UP), send(pair[1][half:], Z_DOWN)


def in_order(block, one, two, three, four):
    return [block, one[1], two[1], three[1], four[0], four[1], three[0], two[0], one[0]]


def split(v):
    hi = v.astype(jnp.bfloat16)
    return hi, (v - hi.astype(jnp.float32)).astype(jnp.bfloat16)


def dot3(a, b, dims):
    def one(p, q):
        return lax.dot_general(p, q, (dims, ((), ())), preferred_element_type=jnp.float32)

    return one(a[0], b[0]) + (one(a[0], b[1]) + one(a[1], b[0]))


def factor_kernel(at, pattern, blocks, factor, p0, p1, p2, p3, pieces):
    row, zl = at[4], at[5]
    cols = blocks.shape[2]
    for child in range(2):
        weight = pattern[child, row].astype(jnp.float32)
        masked = blocks[child] * weight
        factor[:, child * cols : (child + 1) * cols] = masked
        for q in range(4):
            pieces[q, :, child * 64 : (child + 1) * 64] = masked[:, q * 64 : (q + 1) * 64]
    for d, ref in enumerate((p0, p1, p2, p3)):
        ref[...] = pieces[(zl + d) & 3]


def cross_kernel(at, r0, r1, r2, r3, r4t, r4b, r5, r6, r7, o0, o1, o2, o3, s0, s1, s2, s3, t0, t1, t2, t3, hi, lo, total):
    x, y, z, c, zl = at[0], at[1], at[2], at[3], at[5]
    for t, (own, other) in enumerate(((o0, s0), (o1, s1), (o2, s2), (o3, s3))):
        here = slice(t * BLK, (t + 1) * BLK)
        for ref, core in ((own, c), (other, 1 - c)):
            for d in range(4):
                rows = pl.ds(pl.multiple_of((((zl - d) & 3) * 2 + core) * BLK, BLK), BLK)
                hi[rows, here], lo[rows, here] = split(ref[d])
    blocks = [(r0, None), (r1, None), (r2, None), (r3, None), (r4t, r4b), (r5, None), (r6, None), (r7, None)]

    def product(d):
        place = (z + d) & 7
        start = pl.multiple_of((place >> 2) * (4 * BLK), 4 * BLK)
        f = hi[pl.ds(start, 4 * BLK), :], lo[pl.ds(start, 4 * BLK), :]
        first, second = blocks[d]
        value = first[...] if second is None else jnp.concatenate([first[...], second[...]], axis=0)
        return dot3(split(value), f, ((1,), (0,)))

    for p in range(4):
        value = product(p) + product(p + 4)
        rows = pl.ds(pl.multiple_of(((z + p) & 3) * BLK, BLK), BLK)
        for t in range(4):
            total[t, rows, :] = value[:, t * BLK : (t + 1) * BLK]
    for d, ref in enumerate((t0, t1, t2, t3)):
        ref[...] = total[(x - y - d) & 3]


def diag_kernel(at, e0, e1, e2, e3, e4t, e4b, e5, e6, e7, g0, g1, g2, g3, out_send, out_keep, fh, fl, gh, gl, total):
    x, y, z, c = at[0], at[1], at[2], at[3]
    half = BLK // 2
    for ref, d, skip in ((e0, 0, 0), (e1, 1, 0), (e2, 2, 0), (e3, 3, 0), (e4t, 4, 0), (e4b, 4, half), (e5, 5, 0), (e6, 6, 0), (e7, 7, 0)):
        rows = pl.ds(pl.multiple_of(((z + d) & 7) * BLK + skip, half), ref.shape[0])
        fh[rows, :], fl[rows, :] = split(ref[...])
    for d, ref in enumerate((g0, g1, g2, g3)):
        h, l = split(ref[...])
        for child in range(2):
            to = slice(child * 256 + d * 64, child * 256 + (d + 1) * 64)
            of = slice(child * 64, (child + 1) * 64)
            gh[:, to], gl[:, to] = h[:, of], l[:, of]
    for child in range(2):
        here = slice(child * 256, (child + 1) * 256)
        g = gh[:, here], gl[:, here]
        for h in range(2):
            rows = slice(h * 4 * BLK, (h + 1) * 4 * BLK)
            value = dot3(g, (fh[rows, here], fl[rows, here]), ((0,), (0,)))
            for d in range(4):
                total[h, d, child] = value[d * 64 : (d + 1) * 64, :]
    for t in range(4):
        d = (y - x - t) & 3
        out_keep[t] = total[c, d]
        out_send[t] = total[1 - c, d]


def output_kernel(at, pattern, a0, a1, a2, a3, out, pieces):
    row, zl = at[4], at[5]
    for d, ref in enumerate((a0, a1, a2, a3)):
        pieces[(zl - d) & 3] = ref[...]
    for child in range(2):
        weight = pattern[child, row].astype(jnp.float32)
        for q in range(4):
            out[child, :, q * 64 : (q + 1) * 64] = -(pieces[q, :, child * 64 : (child + 1) * 64] * weight)


def local_call(kernel, scalars, operands, outs, scratch, flops, moved):
    vmem, smem = pl.BlockSpec(memory_space=pltpu.VMEM), pl.BlockSpec(memory_space=pltpu.SMEM)
    return pl.pallas_call(
        kernel,
        out_shape=[jax.ShapeDtypeStruct(s, jnp.float32) for s in outs],
        in_specs=[smem] * len(scalars) + [vmem] * len(operands),
        out_specs=[vmem] * len(outs),
        scratch_shapes=scratch,
        cost_estimate=pl.CostEstimate(flops=flops, bytes_accessed=moved, transcendentals=0),
        compiler_params=pltpu.CompilerParams(vmem_limit_bytes=32 * 2**20),
    )(*scalars, *operands)


def body(root_inverse, factor_blocks, pattern, diag_inverse):
    row, col = lax.axis_index("row"), lax.axis_index("col")
    x, zl, c, y, zh = row >> 3, (row >> 1) & 3, row & 1, col >> 1, col & 1
    at = jnp.stack([x, y, zh * 4 + zl, c, row, zl]).astype(jnp.int32)
    cols = factor_blocks.shape[2]
    piece = (BLK, BLK)

    root1 = step((root_inverse, root_inverse))
    factor, *strips = local_call(
        factor_kernel, [at, pattern], [factor_blocks], [(BLK, 2 * cols)] + [piece] * 4, [pltpu.VMEM((4,) + piece, jnp.float32)], 2**16, 2**20
    )
    column = jnp.stack([strips[0]] + [send(strips[d], Z_MOVES[d]) for d in (1, 2, 3)])
    own = [send(column, CROSS[t]) for t in range(4)]
    other = [send(v, CORE) for v in own]
    around1 = step((factor, factor))
    root2 = step(root1)
    root2, around1 = lax.optimization_barrier((root2, around1))
    root3 = step(root2)
    root4 = last_step(root3)
    wide = pltpu.VMEM((8 * BLK, 2 * cols), jnp.bfloat16)
    parts = local_call(
        cross_kernel,
        [at],
        in_order(root_inverse, root1, root2, root3, root4) + own + other,
        [(4 * BLK, BLK)] * 4,
        [wide, wide, pltpu.VMEM((4, 4 * BLK, BLK), jnp.float32)],
        6 * 512 * 1024 * 512,
        6 * 2**20,
    )
    around2 = step(around1)
    g = parts[0] + send(parts[1], Y_MOVES[1]) + send(parts[2], Y_MOVES[2]) + send(parts[3], Y_MOVES[3])
    around3 = step(around2)
    gathered = [g] + [send(g, Y_MOVES[d]) for d in (1, 2, 3)]
    around4 = last_step(around3)

    out_send, out_keep = local_call(
        diag_kernel,
        [at],
        in_order(factor, around1, around2, around3, around4) + gathered,
        [(4, 2, BLK // 2, cols)] * 2,
        [wide, wide]
        + [pltpu.VMEM((4 * BLK, 2 * cols), jnp.bfloat16)] * 2
        + [pltpu.VMEM((2, 4, 2, BLK // 2, cols), jnp.float32)],
        6 * 512 * 512 * 512,
        6 * 2**20,
    )
    g_rows = g.reshape((4,) + piece)
    rows = [lax.dynamic_index_in_dim(g_rows, (zl + d) & 3, 0, keepdims=False) for d in range(4)]
    rows = [rows[0]] + [send(rows[d], Z_MOVES[d]) for d in (1, 2, 3)]
    swapped = send(out_send, CORE)
    (cross,) = local_call(output_kernel, [at, pattern], rows, [(2, BLK, cols)], [pltpu.VMEM((4,) + piece, jnp.float32)], 2**16, 2**20)
    part = out_keep + swapped
    last = part[0] + send(part[1], X_MOVES[1]) + send(part[2], X_MOVES[2]) + send(part[3], X_MOVES[3])
    last, cross = lax.optimization_barrier((last, cross))
    diag = diag_inverse + send(last, HOME)
    return cross, diag


def solution(mesh):
    placed = (P("row", "col"), P(None, "row", "col"), P(), P(None, "row", "col"))
    return jax.shard_map(
        body,
        mesh=mesh,
        in_specs=placed,
        out_specs=(P(None, "row", "col"), P(None, "row", "col")),
        check_vma=False,
    )
```

```python
import jax
import jax.numpy as jnp
from jax import lax
from jax.experimental import pallas as pl
from jax.experimental.pallas import tpu as pltpu
from jax.sharding import PartitionSpec as P

AX = ("row", "col")
BLK = 128
NX, NZL, NC, NY, NZH = 4, 4, 2, 4, 2


def linear(x, zl, c, y, zh):
    return (((x * NZL + zl) * NC + c) * NY + y) * NZH + zh


def moves(target):
    pairs = []
    for x in range(NX):
        for zl in range(NZL):
            for c in range(NC):
                for y in range(NY):
                    for zh in range(NZH):
                        pairs.append((linear(x, zl, c, y, zh), linear(*target(x, zl, c, y, zh))))
    return pairs


def z_step(d):
    def target(x, zl, c, y, zh):
        z = (zh * NZL + zl + d) % (NZL * NZH)
        return x, z % NZL, c, y, z // NZL

    return moves(target)


Z_UP, Z_DOWN = z_step(1), z_step(-1)
Z_MOVES = [moves(lambda x, zl, c, y, zh, d=d: (x, (zl + d) % NZL, c, y, zh)) for d in range(NZL)]
X_MOVES = [moves(lambda x, zl, c, y, zh, d=d: ((x + d) % NX, zl, c, y, zh)) for d in range(NX)]
Y_MOVES = [moves(lambda x, zl, c, y, zh, d=d: (x, zl, c, (y + d) % NY, zh)) for d in range(NY)]
CORE = moves(lambda x, zl, c, y, zh: (x, zl, 1 - c, y, zh))
CROSS = [moves(lambda x, zl, c, y, zh, t=t: ((y + t) % NX, zl, c, x, zh)) for t in range(NX)]
HOME = moves(lambda x, zl, c, y, zh: (x, (zh * NZL + zl) >> 1, zl & 1, y, c))


def send(value, pairs):
    return lax.ppermute(value, AX, pairs)


def step(pair):
    return send(pair[0], Z_UP), send(pair[1], Z_DOWN)


def last_step(pair):
    half = pair[0].shape[0] // 2
    return send(pair[0][:half], Z_UP), send(pair[1][half:], Z_DOWN)


def in_order(block, one, two, three, four):
    return [block, one[1], two[1], three[1], four[0], four[1], three[0], two[0], one[0]]


def split(v):
    hi = v.astype(jnp.bfloat16)
    return hi, (v - hi.astype(jnp.float32)).astype(jnp.bfloat16)


def dot3(a, b, dims):
    def one(p, q):
        return lax.dot_general(p, q, (dims, ((), ())), preferred_element_type=jnp.float32)

    return one(a[0], b[0]) + (one(a[0], b[1]) + one(a[1], b[0]))


def factor_kernel(at, pattern, blocks, factor, p0, p1, p2, p3, pieces):
    row, zl = at[4], at[5]
    cols = blocks.shape[2]
    for child in range(2):
        weight = pattern[child, row].astype(jnp.float32)
        masked = blocks[child] * weight
        factor[:, child * cols : (child + 1) * cols] = masked
        for q in range(4):
            pieces[q, :, child * 64 : (child + 1) * 64] = masked[:, q * 64 : (q + 1) * 64]
    for d, ref in enumerate((p0, p1, p2, p3)):
        ref[...] = pieces[(zl + d) & 3]


def cross_kernel(at, r0, r1, r2, r3, r4t, r4b, r5, r6, r7, o0, o1, o2, o3, s0, s1, s2, s3, t0, t1, t2, t3, hi, lo, total):
    x, y, z, c, zl = at[0], at[1], at[2], at[3], at[5]
    for t, (own, other) in enumerate(((o0, s0), (o1, s1), (o2, s2), (o3, s3))):
        here = slice(t * BLK, (t + 1) * BLK)
        for ref, core in ((own, c), (other, 1 - c)):
            for d in range(4):
                rows = pl.ds(pl.multiple_of((((zl - d) & 3) * 2 + core) * BLK, BLK), BLK)
                hi[rows, here], lo[rows, here] = split(ref[d])
    blocks = [(r0, None), (r1, None), (r2, None), (r3, None), (r4t, r4b), (r5, None), (r6, None), (r7, None)]

    def product(d):
        place = (z + d) & 7
        start = pl.multiple_of((place >> 2) * (4 * BLK), 4 * BLK)
        f = hi[pl.ds(start, 4 * BLK), :], lo[pl.ds(start, 4 * BLK), :]
        first, second = blocks[d]
        value = first[...] if second is None else jnp.concatenate([first[...], second[...]], axis=0)
        return dot3(split(value), f, ((1,), (0,)))

    for p in range(4):
        value = product(p) + product(p + 4)
        rows = pl.ds(pl.multiple_of(((z + p) & 3) * BLK, BLK), BLK)
        for t in range(4):
            total[t, rows, :] = value[:, t * BLK : (t + 1) * BLK]
    for d, ref in enumerate((t0, t1, t2, t3)):
        ref[...] = total[(x - y - d) & 3]


def diag_kernel(at, e0, e1, e2, e3, e4t, e4b, e5, e6, e7, g0, g1, g2, g3, out_send, out_keep, fh, fl, gh, gl, total):
    x, y, z, c = at[0], at[1], at[2], at[3]
    half = BLK // 2
    for ref, d, skip in ((e0, 0, 0), (e1, 1, 0), (e2, 2, 0), (e3, 3, 0), (e4t, 4, 0), (e4b, 4, half), (e5, 5, 0), (e6, 6, 0), (e7, 7, 0)):
        rows = pl.ds(pl.multiple_of(((z + d) & 7) * BLK + skip, half), ref.shape[0])
        fh[rows, :], fl[rows, :] = split(ref[...])
    for d, ref in enumerate((g0, g1, g2, g3)):
        h, l = split(ref[...])
        for child in range(2):
            to = slice(child * 256 + d * 64, child * 256 + (d + 1) * 64)
            of = slice(child * 64, (child + 1) * 64)
            gh[:, to], gl[:, to] = h[:, of], l[:, of]
    for child in range(2):
        here = slice(child * 256, (child + 1) * 256)
        g = gh[:, here], gl[:, here]
        for h in range(2):
            rows = slice(h * 4 * BLK, (h + 1) * 4 * BLK)
            value = dot3(g, (fh[rows, here], fl[rows, here]), ((0,), (0,)))
            for d in range(4):
                total[h, d, child] = value[d * 64 : (d + 1) * 64, :]
    for t in range(4):
        d = (y - x - t) & 3
        out_keep[t] = total[c, d]
        out_send[t] = total[1 - c, d]


def output_kernel(at, pattern, a0, a1, a2, a3, out, pieces):
    row, zl = at[4], at[5]
    for d, ref in enumerate((a0, a1, a2, a3)):
        pieces[(zl - d) & 3] = ref[...]
    for child in range(2):
        weight = pattern[child, row].astype(jnp.float32)
        for q in range(4):
            out[child, :, q * 64 : (q + 1) * 64] = -(pieces[q, :, child * 64 : (child + 1) * 64] * weight)


def local_call(kernel, scalars, operands, outs, scratch, flops, moved):
    vmem, smem = pl.BlockSpec(memory_space=pltpu.VMEM), pl.BlockSpec(memory_space=pltpu.SMEM)
    return pl.pallas_call(
        kernel,
        out_shape=[jax.ShapeDtypeStruct(s, jnp.float32) for s in outs],
        in_specs=[smem] * len(scalars) + [vmem] * len(operands),
        out_specs=[vmem] * len(outs),
        scratch_shapes=scratch,
        cost_estimate=pl.CostEstimate(flops=flops, bytes_accessed=moved, transcendentals=0),
        compiler_params=pltpu.CompilerParams(vmem_limit_bytes=32 * 2**20),
    )(*scalars, *operands)


def body(root_inverse, factor_blocks, pattern, diag_inverse):
    row, col = lax.axis_index("row"), lax.axis_index("col")
    x, zl, c, y, zh = row >> 3, (row >> 1) & 3, row & 1, col >> 1, col & 1
    at = jnp.stack([x, y, zh * 4 + zl, c, row, zl]).astype(jnp.int32)
    cols = factor_blocks.shape[2]
    piece = (BLK, BLK)

    root1 = step((root_inverse, root_inverse))
    factor, *strips = local_call(
        factor_kernel, [at, pattern], [factor_blocks], [(BLK, 2 * cols)] + [piece] * 4, [pltpu.VMEM((4,) + piece, jnp.float32)], 2**16, 2**20
    )
    strips[3], root1 = lax.optimization_barrier((strips[3], root1))
    column = jnp.stack([strips[0]] + [send(strips[d], Z_MOVES[d]) for d in (1, 2, 3)])
    own = [send(column, CROSS[t]) for t in range(4)]
    other = [send(v, CORE) for v in own]
    around1 = step((factor, factor))
    root2 = step(root1)
    root3 = step(root2)
    root4 = last_step(root3)
    wide = pltpu.VMEM((8 * BLK, 2 * cols), jnp.bfloat16)
    parts = local_call(
        cross_kernel,
        [at],
        in_order(root_inverse, root1, root2, root3, root4) + own + other,
        [(4 * BLK, BLK)] * 4,
        [wide, wide, pltpu.VMEM((4, 4 * BLK, BLK), jnp.float32)],
        6 * 512 * 1024 * 512,
        6 * 2**20,
    )
    around2 = step(around1)
    g = parts[0] + send(parts[1], Y_MOVES[1]) + send(parts[2], Y_MOVES[2]) + send(parts[3], Y_MOVES[3])
    around3 = step(around2)
    gathered = [g] + [send(g, Y_MOVES[d]) for d in (1, 2, 3)]
    around4 = last_step(around3)

    out_send, out_keep = local_call(
        diag_kernel,
        [at],
        in_order(factor, around1, around2, around3, around4) + gathered,
        [(4, 2, BLK // 2, cols)] * 2,
        [wide, wide]
        + [pltpu.VMEM((4 * BLK, 2 * cols), jnp.bfloat16)] * 2
        + [pltpu.VMEM((2, 4, 2, BLK // 2, cols), jnp.float32)],
        6 * 512 * 512 * 512,
        6 * 2**20,
    )
    g_rows = g.reshape((4,) + piece)
    rows = [lax.dynamic_index_in_dim(g_rows, (zl + d) & 3, 0, keepdims=False) for d in range(4)]
    rows = [rows[0]] + [send(rows[d], Z_MOVES[d]) for d in (1, 2, 3)]
    swapped = send(out_send, CORE)
    (cross,) = local_call(output_kernel, [at, pattern], rows, [(2, BLK, cols)], [pltpu.VMEM((4,) + piece, jnp.float32)], 2**16, 2**20)
    part = out_keep + swapped
    last = part[0] + send(part[1], X_MOVES[1]) + send(part[2], X_MOVES[2]) + send(part[3], X_MOVES[3])
    last, cross = lax.optimization_barrier((last, cross))
    diag = diag_inverse + send(last, HOME)
    return cross, diag


def solution(mesh):
    placed = (P("row", "col"), P(None, "row", "col"), P(), P(None, "row", "col"))
    return jax.shard_map(
        body,
        mesh=mesh,
        in_specs=placed,
        out_specs=(P(None, "row", "col"), P(None, "row", "col")),
        check_vma=False,
    )
```

```python
import jax
import jax.numpy as jnp
from jax import lax
from jax.experimental import pallas as pl
from jax.experimental.pallas import tpu as pltpu
from jax.sharding import PartitionSpec as P

AX = ("row", "col")
BLK = 128
NX, NZL, NC, NY, NZH = 4, 4, 2, 4, 2


def linear(x, zl, c, y, zh):
    return (((x * NZL + zl) * NC + c) * NY + y) * NZH + zh


def moves(target):
    pairs = []
    for x in range(NX):
        for zl in range(NZL):
            for c in range(NC):
                for y in range(NY):
                    for zh in range(NZH):
                        pairs.append((linear(x, zl, c, y, zh), linear(*target(x, zl, c, y, zh))))
    return pairs


def z_step(d):
    def target(x, zl, c, y, zh):
        z = (zh * NZL + zl + d) % (NZL * NZH)
        return x, z % NZL, c, y, z // NZL

    return moves(target)


Z_UP, Z_DOWN = z_step(1), z_step(-1)
Z_MOVES = [moves(lambda x, zl, c, y, zh, d=d: (x, (zl + d) % NZL, c, y, zh)) for d in range(NZL)]
X_MOVES = [moves(lambda x, zl, c, y, zh, d=d: ((x + d) % NX, zl, c, y, zh)) for d in range(NX)]
Y_MOVES = [moves(lambda x, zl, c, y, zh, d=d: (x, zl, c, (y + d) % NY, zh)) for d in range(NY)]
CORE = moves(lambda x, zl, c, y, zh: (x, zl, 1 - c, y, zh))
CROSS = [moves(lambda x, zl, c, y, zh, t=t: ((y + t) % NX, zl, c, x, zh)) for t in range(NX)]
HOME = moves(lambda x, zl, c, y, zh: (x, (zh * NZL + zl) >> 1, zl & 1, y, c))


def send(value, pairs):
    return lax.ppermute(value, AX, pairs)


def step(pair):
    return send(pair[0], Z_UP), send(pair[1], Z_DOWN)


def last_step(pair):
    half = pair[0].shape[0] // 2
    return send(pair[0][:half], Z_UP), send(pair[1][half:], Z_DOWN)


def in_order(block, one, two, three, four):
    return [block, one[1], two[1], three[1], four[0], four[1], three[0], two[0], one[0]]


def split(v):
    hi = v.astype(jnp.bfloat16)
    return hi, (v - hi.astype(jnp.float32)).astype(jnp.bfloat16)


def dot3(a, b, dims):
    def one(p, q):
        return lax.dot_general(p, q, (dims, ((), ())), preferred_element_type=jnp.float32)

    return one(a[0], b[0]) + (one(a[0], b[1]) + one(a[1], b[0]))


def factor_kernel(at, pattern, blocks, factor, p0, p1, p2, p3, pieces):
    row, zl = at[4], at[5]
    cols = blocks.shape[2]
    for child in range(2):
        weight = pattern[child, row].astype(jnp.float32)
        masked = blocks[child] * weight
        factor[:, child * cols : (child + 1) * cols] = masked
        for q in range(4):
            pieces[q, :, child * 64 : (child + 1) * 64] = masked[:, q * 64 : (q + 1) * 64]
    for d, ref in enumerate((p0, p1, p2, p3)):
        ref[...] = pieces[(zl + d) & 3]


def cross_kernel(at, r0, r1, r2, r3, r4t, r4b, r5, r6, r7, o0, o1, o2, o3, s0, s1, s2, s3, t0, t1, t2, t3, hi, lo, total):
    x, y, z, c, zl = at[0], at[1], at[2], at[3], at[5]
    for t, (own, other) in enumerate(((o0, s0), (o1, s1), (o2, s2), (o3, s3))):
        here = slice(t * BLK, (t + 1) * BLK)
        for ref, core in ((own, c), (other, 1 - c)):
            for d in range(4):
                rows = pl.ds(pl.multiple_of((((zl - d) & 3) * 2 + core) * BLK, BLK), BLK)
                hi[rows, here], lo[rows, here] = split(ref[d])
    blocks = [(r0, None), (r1, None), (r2, None), (r3, None), (r4t, r4b), (r5, None), (r6, None), (r7, None)]

    def product(d):
        place = (z + d) & 7
        start = pl.multiple_of((place >> 2) * (4 * BLK), 4 * BLK)
        f = hi[pl.ds(start, 4 * BLK), :], lo[pl.ds(start, 4 * BLK), :]
        first, second = blocks[d]
        value = first[...] if second is None else jnp.concatenate([first[...], second[...]], axis=0)
        return dot3(split(value), f, ((1,), (0,)))

    for p in range(4):
        value = product(p) + product(p + 4)
        rows = pl.ds(pl.multiple_of(((z + p) & 3) * BLK, BLK), BLK)
        for t in range(4):
            total[t, rows, :] = value[:, t * BLK : (t + 1) * BLK]
    for d, ref in enumerate((t0, t1, t2, t3)):
        ref[...] = total[(x - y - d) & 3]


def diag_kernel(at, e0, e1, e2, e3, e4t, e4b, e5, e6, e7, g0, g1, g2, g3, out_send, out_keep, fh, fl, gh, gl, total):
    x, y, z, c = at[0], at[1], at[2], at[3]
    half = BLK // 2
    for ref, d, skip in ((e0, 0, 0), (e1, 1, 0), (e2, 2, 0), (e3, 3, 0), (e4t, 4, 0), (e4b, 4, half), (e5, 5, 0), (e6, 6, 0), (e7, 7, 0)):
        rows = pl.ds(pl.multiple_of(((z + d) & 7) * BLK + skip, half), ref.shape[0])
        fh[rows, :], fl[rows, :] = split(ref[...])
    for d, ref in enumerate((g0, g1, g2, g3)):
        h, l = split(ref[...])
        for child in range(2):
            to = slice(child * 256 + d * 64, child * 256 + (d + 1) * 64)
            of = slice(child * 64, (child + 1) * 64)
            gh[:, to], gl[:, to] = h[:, of], l[:, of]
    for child in range(2):
        here = slice(child * 256, (child + 1) * 256)
        g = gh[:, here], gl[:, here]
        for h in range(2):
            rows = slice(h * 4 * BLK, (h + 1) * 4 * BLK)
            value = dot3(g, (fh[rows, here], fl[rows, here]), ((0,), (0,)))
            for d in range(4):
                total[h, d, child] = value[d * 64 : (d + 1) * 64, :]
    for t in range(4):
        d = (y - x - t) & 3
        out_keep[t] = total[c, d]
        out_send[t] = total[1 - c, d]


def output_kernel(at, pattern, a0, a1, a2, a3, out, pieces):
    row, zl = at[4], at[5]
    for d, ref in enumerate((a0, a1, a2, a3)):
        pieces[(zl - d) & 3] = ref[...]
    for child in range(2):
        weight = pattern[child, row].astype(jnp.float32)
        for q in range(4):
            out[child, :, q * 64 : (q + 1) * 64] = -(pieces[q, :, child * 64 : (child + 1) * 64] * weight)


def local_call(kernel, scalars, operands, outs, scratch, flops, moved):
    vmem, smem = pl.BlockSpec(memory_space=pltpu.VMEM), pl.BlockSpec(memory_space=pltpu.SMEM)
    return pl.pallas_call(
        kernel,
        out_shape=[jax.ShapeDtypeStruct(s, jnp.float32) for s in outs],
        in_specs=[smem] * len(scalars) + [vmem] * len(operands),
        out_specs=[vmem] * len(outs),
        scratch_shapes=scratch,
        cost_estimate=pl.CostEstimate(flops=flops, bytes_accessed=moved, transcendentals=0),
        compiler_params=pltpu.CompilerParams(vmem_limit_bytes=32 * 2**20),
    )(*scalars, *operands)


def body(root_inverse, factor_blocks, pattern, diag_inverse):
    row, col = lax.axis_index("row"), lax.axis_index("col")
    x, zl, c, y, zh = row >> 3, (row >> 1) & 3, row & 1, col >> 1, col & 1
    at = jnp.stack([x, y, zh * 4 + zl, c, row, zl]).astype(jnp.int32)
    cols = factor_blocks.shape[2]
    piece = (BLK, BLK)

    root1 = step((root_inverse, root_inverse))
    factor, *strips = local_call(
        factor_kernel, [at, pattern], [factor_blocks], [(BLK, 2 * cols)] + [piece] * 4, [pltpu.VMEM((4,) + piece, jnp.float32)], 2**16, 2**20
    )
    strips[3], root1 = lax.optimization_barrier((strips[3], root1))
    column = jnp.stack([strips[0]] + [send(strips[d], Z_MOVES[d]) for d in (1, 2, 3)])
    own = [send(column, CROSS[t]) for t in (3, 2, 1, 0)][::-1]
    other = [send(v, CORE) for v in own[::-1]][::-1]
    around1 = step((factor, factor))
    root2 = step(root1)
    root3 = step(root2)
    root4 = last_step(root3)
    wide = pltpu.VMEM((8 * BLK, 2 * cols), jnp.bfloat16)
    parts = local_call(
        cross_kernel,
        [at],
        in_order(root_inverse, root1, root2, root3, root4) + own + other,
        [(4 * BLK, BLK)] * 4,
        [wide, wide, pltpu.VMEM((4, 4 * BLK, BLK), jnp.float32)],
        6 * 512 * 1024 * 512,
        6 * 2**20,
    )
    around2 = step(around1)
    g = parts[0] + send(parts[1], Y_MOVES[1]) + send(parts[2], Y_MOVES[2]) + send(parts[3], Y_MOVES[3])
    around3 = step(around2)
    gathered = [g] + [send(g, Y_MOVES[d]) for d in (1, 2, 3)]
    around4 = last_step(around3)

    out_send, out_keep = local_call(
        diag_kernel,
        [at],
        in_order(factor, around1, around2, around3, around4) + gathered,
        [(4, 2, BLK // 2, cols)] * 2,
        [wide, wide]
        + [pltpu.VMEM((4 * BLK, 2 * cols), jnp.bfloat16)] * 2
        + [pltpu.VMEM((2, 4, 2, BLK // 2, cols), jnp.float32)],
        6 * 512 * 512 * 512,
        6 * 2**20,
    )
    g_rows = g.reshape((4,) + piece)
    rows = [lax.dynamic_index_in_dim(g_rows, (zl + d) & 3, 0, keepdims=False) for d in range(4)]
    rows = [rows[0]] + [send(rows[d], Z_MOVES[d]) for d in (1, 2, 3)]
    swapped = send(out_send, CORE)
    part = out_keep + swapped
    last = part[0] + send(part[1], X_MOVES[1]) + send(part[2], X_MOVES[2]) + send(part[3], X_MOVES[3])
    last, rows[1], rows[2] = lax.optimization_barrier((last, rows[1], rows[2]))
    diag = diag_inverse + send(last, HOME)
    (cross,) = local_call(output_kernel, [at, pattern], rows, [(2, BLK, cols)], [pltpu.VMEM((4,) + piece, jnp.float32)], 2**16, 2**20)
    return cross, diag


def solution(mesh):
    placed = (P("row", "col"), P(None, "row", "col"), P(), P(None, "row", "col"))
    return jax.shard_map(
        body,
        mesh=mesh,
        in_specs=placed,
        out_specs=(P(None, "row", "col"), P(None, "row", "col")),
        check_vma=False,
    )
```
